32 devices in a mesh: own: 16 (over z, y, x), rep: 2 (over core).
Axes of the slice: x: 2, y: 2, z: 4, core: 2. Of those that a mesh axis runs over, the one named last changes fastest.
Arguments:
- tokens: bfloat16 [4096, 2560], P(('own', 'rep')), may hold values from -6 to 6
- cotangent: bfloat16 [4096, 2560], P(('own', 'rep')), may hold values from -6 to 6
- route: int32 [4096, 6], P(('own', 'rep')), may hold values from 0 to 159, all different within a row; in each aligned block of 128 rows (0 to 127, 128 to 255, ...) at most 6 rows name the same one
- gate_index: int32 [4096, 6], P(('own', 'rep')), may hold values from 0 to 255
- gate_table: float32 [256], replicated, may hold values from 0.1 to 1
- w_gate: bfloat16 [4096, 2560], P(('own', 'rep')), may hold values from -0.125 to 0.125
- w_up: bfloat16 [4096, 2560], P(('own', 'rep')), may hold values from -0.125 to 0.125
- w_down: bfloat16 [4096, 2560], P(('own', 'rep')), may hold values from -0.1875 to 0.1875
Outputs:
- grad_tokens: bfloat16 [4096, 2560], P(('own', 'rep'))
- grad_w_gate: float32 [4096, 2560], P(('own', 'rep'))
- grad_w_up: float32 [4096, 2560], P(('own', 'rep'))
- grad_w_down: float32 [4096, 2560], P(('own', 'rep'))
The draws below stay inside these ranges and needn't reach their ends.
Inputs may be any that keep to these rules, and one draw needn't show every extreme that they name: `route`: each row names 6 different experts. Among the rows of one device no expert is named by more than 6 rows, and in some device some expert is named by exactly 6.
All inputs are finite; a program needn't handle non-finite values.
Results may differ from the reference program's by a relative error of at most 0.015.
Values may be sent and summed in bfloat16 or wider, within the bound.
A program may use at most 64 MiB of HBM per device.

```python
import math
import jax
import jax.numpy as jnp
import numpy as np
from jax import lax

D = 2560
FF = 1024
EXPERTS = 160
TOP = 6
SPLIT = 4
GTAB = 256
TOK_DEV = 128
CAP = 6
EW = 4
TOKENS = 4096
N_OWN = 16
N_REP = 2


def touch_ends(values, rng, smallest, top_value):
    extent = values.shape
    index_at = [jax.random.randint(jax.random.fold_in(rng, axis), (), 0, extent[axis]) for axis in range(len(extent))]
    values = values.at[tuple(index_at)].set(smallest)
    longest = extent.index(max(extent))
    index_at[longest] = (index_at[longest] + 1) % extent[longest]
    return values.at[tuple(index_at)].set(top_value)


def block_levels(rng, extent, split, least, top_value):
    def one(dim, parts):
        steps = jax.random.uniform(jax.random.fold_in(jax.random.fold_in(rng, 6), dim), (parts,), jnp.float32, least / len(split), top_value / len(split))
        return jnp.repeat(jnp.exp(steps), extent[dim] // parts).reshape((-1,) + (1,) * (len(extent) - dim - 1))

    loudness = one(*split[0])
    for cut in split[1:]:
        loudness = loudness * one(*cut)
    return loudness


def shared_out(own_key, own, number, rows, number_of, top, reach, skew):
    sequence = jax.random.permutation(own_key, number_of)
    heavy_load, usual = shares(number_of, rows * top, reach, skew, True), shares(number_of, rows * top, reach, skew, False)
    places = jnp.arange(number_of)

    def named(tallies, rotation):
        used = int((tallies > 0).sum())
        fixed = max(1, used // 4)
        moved = fixed + (places - fixed + rotation * (used - fixed)) % max(1, number_of - fixed)
        return jnp.zeros((number_of,), jnp.int32).at[sequence[jnp.where(places < fixed, places, moved)]].set(jnp.asarray(tallies, jnp.int32))

    tallies = jnp.where(number % 4 == 0, named(heavy_load, number // 4), named(usual, number - number // 4 - 1))
    mixed = jax.random.permutation(jax.random.fold_in(own, 3), number_of)
    donor, receiver = mixed[0:number_of // 2 * 2:2], mixed[1:number_of // 2 * 2:2]
    slack = jnp.minimum(tallies[donor] - 1, reach - tallies[receiver]) // 2
    slack = jnp.where((donor == sequence[0]) | (receiver == sequence[0]) | (tallies[receiver] == 0), 0, jnp.maximum(slack, 0))
    moved = jax.random.randint(jax.random.fold_in(own, 4), (number_of // 2,), 0, 1 << 20) % (slack + 1)
    tallies = tallies.at[donor].add(-moved).at[receiver].add(moved)
    labels = jnp.searchsorted(jnp.cumsum(tallies), jnp.arange(rows * top), side="right").astype(jnp.int32)
    grid = labels.reshape(top, rows).T
    grid = grid[jax.random.permutation(jax.random.fold_in(own, 1), rows)]
    rotation = jax.random.randint(jax.random.fold_in(own, 2), (rows, 1), 0, top)
    return jnp.take_along_axis(grid, (jnp.arange(top)[None, :] + rotation) % top, axis=1)


def shares(number_of, total, reach, lean, full):
    portions = [(1 << 20) // math.isqrt(rank ** lean) + 1 for rank in range(1, number_of + 1)]
    largest = reach if full else min(reach, max(-(-total // number_of), total * portions[0] // sum(portions)))
    least = 1 if total - largest >= number_of - 1 else 0
    counts, spare = [largest] + [least] * (number_of - 1), total - largest - least * (number_of - 1)
    while spare > 0:
        candidates = [i for i in range(1, number_of) if counts[i] < largest] or [i for i in range(1, number_of) if counts[i] < reach]
        pool, budget = sum([portions[i] for i in candidates]), spare
        for i in candidates:
            extra = min(reach - counts[i], max(1, budget * portions[i] // pool), spare)
            counts[i] = counts[i] + extra
            spare = spare - extra
    return np.array(counts)


def gaussian(own_key, dims, spread, reach, pieces=(), kind=jnp.bfloat16):
    drawn = jax.random.normal(own_key, dims, jnp.float32) * spread
    if len(pieces) > 0:
        drawn = block_levels(own_key, dims, pieces, -0.22, 0.18) * drawn
    return jnp.clip(drawn, min=-reach, max=reach).astype(kind)


def setup_inputs(seed: int = 0) -> dict:
    streams_of = jax.random.split(jax.random.key(seed), 9)
    tokens = gaussian(streams_of[0], (TOKENS, D), 1.0, 6.0, ((0, 32),))
    cotangent = gaussian(streams_of[1], (TOKENS, D), 1.0, 6.0, ((0, 32),))
    route_keys = jax.random.split(jax.random.fold_in(streams_of[2], 1), TOKENS // TOK_DEV)
    route_turns = jax.random.permutation(jax.random.fold_in(streams_of[2], 3), TOKENS // TOK_DEV)
    route = jax.vmap(lambda own, number: shared_out(jax.random.fold_in(streams_of[2], 2), own, number, TOK_DEV, EXPERTS, TOP, CAP, 2))(route_keys, route_turns).reshape((TOKENS, TOP))
    gate_index = touch_ends(jax.random.randint(streams_of[3], (TOKENS, TOP), 0, GTAB), jax.random.fold_in(streams_of[3], 1), 0, GTAB - 1).astype(jnp.int32)
    gate_table = jnp.clip(jnp.exp(jax.random.uniform(streams_of[4], (GTAB,), jnp.float32, math.log(0.1), math.log(1.0))), 0.1, 1.0)
    w_gate = gaussian(streams_of[5], (EW * FF, D), D ** -0.5, 0.125, ((0, 32),))
    w_up = gaussian(streams_of[6], (EW * FF, D), D ** -0.5, 0.125, ((0, 32),))
    w_down = gaussian(streams_of[7], (EW * FF, D), FF ** -0.5, 0.1875, ((0, 32),))
    return dict(tokens=tokens, cotangent=cotangent, route=route, gate_index=gate_index, gate_table=gate_table, w_gate=w_gate, w_up=w_up, w_down=w_down)


def silu_parts(pre_gate):
    sigmoid_value = jax.nn.sigmoid(pre_gate)
    return pre_gate * sigmoid_value, sigmoid_value * (1.0 + pre_gate * (1.0 - sigmoid_value))


def rep_partials(left_rows, right_rows):
    left_grid = left_rows.reshape(N_OWN, N_REP, CAP, left_rows.shape[-1]).astype(jnp.float32)
    right_grid = right_rows.reshape(N_OWN, N_REP, CAP, right_rows.shape[-1]).astype(jnp.float32)
    partials = jnp.einsum('orcf,orcd->rfd', left_grid, right_grid, precision=lax.Precision.HIGHEST)
    return lax.optimization_barrier(partials.astype(jnp.bfloat16)).astype(jnp.float32).sum(axis=0)


def block_sums(delta_rows, panel):
    delta_blocks = delta_rows.astype(jnp.float32).reshape(delta_rows.shape[0], SPLIT, FF // SPLIT)
    panel_blocks = panel.astype(jnp.float32).reshape(SPLIT, FF // SPLIT, D)
    return jnp.einsum('rsf,sfd->rsd', delta_blocks, panel_blocks, precision=lax.Precision.HIGHEST)


def reference(tokens, cotangent, route, gate_index, gate_table, w_gate, w_up, w_down):
    devices_all = N_OWN * N_REP
    window = N_OWN // SPLIT
    gate_values = gate_table[gate_index].reshape(devices_all, TOK_DEV * TOP)
    routes = route.reshape(devices_all, TOK_DEV * TOP)
    expert_ids = jnp.arange(window, dtype=jnp.int32)
    slot_ids = jnp.arange(CAP, dtype=jnp.int32)
    is_named = (routes[:, :, None] == expert_ids[None, None, :]).astype(jnp.int32)
    earlier = jnp.cumsum(is_named, axis=1) - is_named
    slot_hits = (is_named[:, :, :, None] * (earlier[:, :, :, None] == slot_ids[None, None, None, :]).astype(jnp.int32)).astype(jnp.float32)
    select = slot_hits.reshape(devices_all, TOK_DEV, TOP, window, CAP).sum(axis=2)
    slot_gate = jnp.einsum('npec,np->enc', slot_hits, gate_values, precision=lax.Precision.HIGHEST)
    token_rows = tokens.reshape(devices_all, TOK_DEV, D).astype(jnp.float32)
    cot_rows = cotangent.reshape(devices_all, TOK_DEV, D).astype(jnp.float32)
    sent_x = jnp.einsum('ntec,ntd->encd', select, token_rows, precision=lax.Precision.HIGHEST).astype(jnp.bfloat16)
    sent_dy = jnp.einsum('ntec,ntd->encd', select, cot_rows, precision=lax.Precision.HIGHEST)
    sent_cot = (slot_gate[:, :, :, None] * sent_dy).astype(jnp.bfloat16)
    select_first = jnp.transpose(select, (2, 0, 1, 3))
    gate_rows = w_gate.reshape(window, FF, D)
    up_rows = w_up.reshape(window, FF, D)
    down_rows = w_down.reshape(window, FF, D)

    def per_expert(accumulated, inputs):
        expert_x, expert_cot, expert_pick, expert_gate, expert_up, expert_down = inputs
        rows_x = expert_x.reshape(-1, D)
        rows_cot = expert_cot.reshape(-1, D)
        pre_gate = jnp.dot(rows_x, expert_gate.T, preferred_element_type=jnp.float32)
        pre_up = jnp.dot(rows_x, expert_up.T, preferred_element_type=jnp.float32)
        active, slope_value = silu_parts(pre_gate)
        hidden = (active * pre_up).astype(jnp.bfloat16)
        hidden_delta = jnp.dot(rows_cot, expert_down.T, preferred_element_type=jnp.float32)
        gate_delta = (hidden_delta * pre_up * slope_value).astype(jnp.bfloat16)
        up_delta = (hidden_delta * active).astype(jnp.bfloat16)
        block_grad = block_sums(gate_delta, expert_gate) + block_sums(up_delta, expert_up)
        grad_rows = lax.optimization_barrier(block_grad.astype(jnp.bfloat16)).astype(jnp.float32).sum(axis=1)
        accumulated = accumulated + jnp.einsum('ntc,ncd->ntd', expert_pick, grad_rows.reshape(devices_all, CAP, D), precision=lax.Precision.HIGHEST)
        return accumulated, (rep_partials(gate_delta, rows_x), rep_partials(up_delta, rows_x), rep_partials(hidden, rows_cot))

    start_value = jnp.zeros((devices_all, TOK_DEV, D), jnp.float32)
    accumulated, weight_grads = lax.scan(per_expert, start_value, (sent_x, sent_cot, select_first, gate_rows, up_rows, down_rows))
    grad_tokens = accumulated.reshape(devices_all * TOK_DEV, D).astype(jnp.bfloat16)
    return (grad_tokens, weight_grads[0].reshape(window * FF, D), weight_grads[1].reshape(window * FF, D), weight_grads[2].reshape(window * FF, D))
```

```python
import jax
import jax.numpy as jnp
from jax import lax
from jax.sharding import PartitionSpec as P

from jax.experimental import pallas as pl
from jax.experimental.pallas import tpu as pltpu

SPLIT = 4
CAP = 6


def silu_parts(pre_gate):
    sigmoid_value = jax.nn.sigmoid(pre_gate)
    return (pre_gate * sigmoid_value, sigmoid_value * (1.0 + pre_gate * (1.0 - sigmoid_value)))


def panel_terms(rows_x, rows_cot, panel_gate, panel_up, panel_down):
    pre_gate = jnp.dot(rows_x, panel_gate.T, preferred_element_type=jnp.float32)
    pre_up = jnp.dot(rows_x, panel_up.T, preferred_element_type=jnp.float32)
    active, slope_value = silu_parts(pre_gate)
    hidden = (active * pre_up).astype(jnp.bfloat16)
    hidden_delta = jnp.dot(rows_cot, panel_down.T, preferred_element_type=jnp.float32)
    gate_delta = (hidden_delta * pre_up * slope_value).astype(jnp.bfloat16)
    up_delta = (hidden_delta * active).astype(jnp.bfloat16)
    grad_rows = jnp.dot(gate_delta, panel_gate, preferred_element_type=jnp.float32) + jnp.dot(
        up_delta, panel_up, preferred_element_type=jnp.float32
    )
    grad_gate = jnp.dot(gate_delta.T, rows_x, preferred_element_type=jnp.float32)
    grad_up = jnp.dot(up_delta.T, rows_x, preferred_element_type=jnp.float32)
    grad_down = jnp.dot(hidden.T, rows_cot, preferred_element_type=jnp.float32)
    return (grad_rows, grad_gate, grad_up, grad_down)


def per_device(tokens, cotangent, route, gate_index, gate_table, w_gate, w_up, w_down):
    owners = lax.axis_size("own")
    experts_here = owners // SPLIT
    tok_count = tokens.shape[0]
    model_width = tokens.shape[1]
    choices_each = route.shape[1]
    table_hits = (
        gate_index[:, :, None] == jnp.arange(gate_table.shape[0], dtype=jnp.int32)[None, None, :]
    ).astype(jnp.float32)
    gate_values = jnp.sum(table_hits * gate_table[None, None, :], axis=2).reshape(-1)
    is_named = (
        route.reshape(-1)[:, None] == jnp.arange(experts_here, dtype=jnp.int32)[None, :]
    ).astype(jnp.int32)
    pair_ids = jnp.arange(is_named.shape[0], dtype=jnp.int32)
    earlier = jnp.dot(
        (pair_ids[:, None] > pair_ids[None, :]).astype(jnp.bfloat16),
        is_named.astype(jnp.bfloat16),
        preferred_element_type=jnp.float32,
    ).astype(jnp.int32)
    slot_hits = (
        is_named[:, :, None]
        * (earlier[:, :, None] == jnp.arange(CAP, dtype=jnp.int32)[None, None, :]).astype(jnp.int32)
    ).astype(jnp.float32)
    slot_hits = slot_hits.reshape(tok_count * choices_each, experts_here * CAP)
    select = slot_hits.reshape(tok_count, choices_each, experts_here * CAP).sum(axis=1)
    slot_gate = jnp.dot(
        gate_values, slot_hits, precision=lax.Precision.HIGHEST, preferred_element_type=jnp.float32
    )
    picker = select.astype(jnp.bfloat16)
    sent_x = jnp.dot(picker.T, tokens, preferred_element_type=jnp.float32).astype(jnp.bfloat16)
    sent_dy = jnp.dot(picker.T, cotangent, preferred_element_type=jnp.float32)
    sent_cot = (slot_gate[:, None] * sent_dy).astype(jnp.bfloat16)

    def fan_out(slot_rows):
        spread = jnp.broadcast_to(
            slot_rows.reshape(experts_here, 1, CAP, model_width),
            (experts_here, SPLIT, CAP, model_width),
        )
        return spread.reshape(owners, CAP, model_width)

    got_x, got_cot = (
        lax.all_to_all(fan_out(sent_x), "own", split_axis=0, concat_axis=0, tiled=True),
        lax.all_to_all(fan_out(sent_cot), "own", split_axis=0, concat_axis=0, tiled=True),
    )
    rows_x = got_x.reshape(owners * CAP, model_width)
    rows_cot = got_cot.reshape(owners * CAP, model_width)
    full_gate, full_up, full_down = (
        lax.all_gather(w_gate, "rep", axis=0, tiled=True),
        lax.all_gather(w_up, "rep", axis=0, tiled=True),
        lax.all_gather(w_down, "rep", axis=0, tiled=True),
    )
    grad_rows, grad_gate, grad_up, grad_down = panel_terms(
        rows_x, rows_cot, full_gate, full_up, full_down
    )
    block_rows = grad_rows.astype(jnp.bfloat16).reshape(owners, CAP, model_width)
    returned = lax.all_to_all(block_rows, "own", split_axis=0, concat_axis=0, tiled=True)
    per_slot = (
        returned.astype(jnp.float32)
        .reshape(experts_here, SPLIT, CAP, model_width)
        .sum(axis=1)
        .reshape(experts_here * CAP, model_width)
    )
    grad_tokens = jnp.dot(
        select, per_slot, precision=lax.Precision.HIGHEST, preferred_element_type=jnp.float32
    ).astype(jnp.bfloat16)
    stacked = jnp.stack([grad_gate, grad_up, grad_down]).astype(jnp.bfloat16).astype(jnp.float32)
    totals_all = lax.psum(stacked.astype(jnp.bfloat16), "rep").astype(jnp.float32)
    rows_each = stacked.shape[1] // lax.axis_size("rep")
    shares = lax.dynamic_slice_in_dim(totals_all, lax.axis_index("rep") * rows_each, rows_each, 1)
    return (grad_tokens, shares[0], shares[1], shares[2])


MESH = pl.DeviceIdType.MESH
F32 = jnp.float32
BF16 = jnp.bfloat16
SLOT_ROWS = 8
BLOCK = 2 * SLOT_ROWS
PLANE = 4
DEPTH = 4


def flip(value, bit):
    return value + bit - 2 * bit * lax.rem(lax.div(value, bit), 2)


def flipped(value, pattern):
    for bit in (1, 2):
        if pattern & bit:
            value = flip(value, bit)
    return value


def kernel(
    route_ref, gidx_ref, table_ref, tok_hbm, cot_hbm, wg_hbm, wu_hbm, wd_hbm,
    ps_out, sel_out, wgrad_out,
    tok, cot, w, sbuf, rows, delta, acc, pa_s, pa_r, bx_s, bx_r, by_s, by_r,
    cx_s, cx_r, cy_s, cy_r, zs_s, zs_r, wgrad,
    in_sem, out_sem, send_sem, recv_sem,
):
    own = lax.axis_index("own")
    rep = lax.axis_index("rep")
    z = lax.div(own, PLANE)
    s = lax.rem(own, PLANE)
    width = tok.shape[1]
    half = width // 2
    units = wg_hbm.shape[0]

    loads = [
        pltpu.make_async_copy(tok_hbm, tok, in_sem.at[0]),
        pltpu.make_async_copy(cot_hbm, cot, in_sem.at[1]),
        pltpu.make_async_copy(wg_hbm, w.at[pl.ds(0, units)], in_sem.at[2]),
        pltpu.make_async_copy(wu_hbm, w.at[pl.ds(units, units)], in_sem.at[3]),
        pltpu.make_async_copy(wd_hbm, w.at[pl.ds(2 * units, units)], in_sem.at[4]),
    ]
    for load in loads:
        load.start()

    dev_z = [None] + [(flipped(z, k) * PLANE + s, rep) for k in range(1, DEPTH)]
    dev_x = (z * PLANE + flip(s, 1), rep)
    dev_y = (z * PLANE + flip(s, 2), rep)
    dev_p = (own, 1 - rep)
    barrier = pltpu.get_barrier_semaphore()
    for device in dev_z[1:] + [dev_x, dev_y, dev_p]:
        pl.semaphore_signal(barrier, inc=1, device_id=device, device_id_type=MESH)

    number = iter(range(64))

    def remote(src, dst, device):
        i = next(number)
        return pltpu.make_async_remote_copy(
            src_ref=src, dst_ref=dst, send_sem=send_sem.at[i], recv_sem=recv_sem.at[i],
            device_id=device, device_id_type=MESH,
        )

    lo, hi = pl.ds(0, half), pl.ds(half, half)
    ks_all = range(DEPTH)
    c_z = [None] + [remote(sbuf.at[k - 1], rows.at[0, 0, k], dev_z[k]) for k in range(1, DEPTH)]
    c_x = [remote(rows.at[0, 0, k], rows.at[1, 0, k], dev_x) for k in ks_all]
    c_y = [remote(rows.at[0, 0, k], rows.at[2, 0, k], dev_y) for k in ks_all]
    c_rx = [remote(rows.at[2, 0, k, :, hi], rows.at[3, 0, k, :, hi], dev_x) for k in ks_all]
    c_ry = [remote(rows.at[1, 0, k, :, lo], rows.at[3, 0, k, :, lo], dev_y) for k in ks_all]
    c_p = [[remote(rows.at[q, 0, k], rows.at[q, 1, k], dev_p) for k in ks_all] for q in range(PLANE)]
    c_pa = [remote(pa_s.at[q], pa_r.at[q], dev_p) for q in range(PLANE)]
    c_bx = [remote(bx_s.at[q], bx_r.at[q], dev_x) for q in range(2)]
    c_by = [remote(by_s.at[q], by_r.at[q], dev_y) for q in range(2)]
    c_cx = remote(cx_s, cx_r, dev_x)
    c_cy = remote(cy_s, cy_r, dev_y)
    c_zs = [None] + [remote(zs_s.at[k - 1], zs_r.at[k - 1], dev_z[k]) for k in range(1, DEPTH)]

    count, choices = route_ref.shape
    lane = lax.broadcasted_iota(jnp.int32, (1, 128), 1)
    which = lax.div(lane, SLOT_ROWS)
    slot = lax.rem(lane, SLOT_ROWS)
    low, high = lax.rem(which, 2), lax.div(which, 2)
    z_low, z_high = lax.rem(z, 2), lax.div(z, 2)
    expert = (low + z_low - 2 * low * z_low) + 2 * (high + z_high - 2 * high * z_high)
    expert = jnp.where(which < DEPTH, expert, -1)
    named = jnp.zeros((count, 128), F32)
    entry = jnp.zeros((count, 128), F32)
    for choice in range(choices):
        hit = route_ref[:, choice : choice + 1] == expert
        named = named + jnp.where(hit, 1.0, 0.0)
        entry = entry + jnp.where(hit, gidx_ref[:, choice : choice + 1].astype(F32), 0.0)
    below = (
        lax.broadcasted_iota(jnp.int32, (count, count), 0)
        > lax.broadcasted_iota(jnp.int32, (count, count), 1)
    )
    earlier = jnp.dot(
        jnp.where(below, 1.0, 0.0).astype(BF16), named.astype(BF16), preferred_element_type=F32
    )
    select = jnp.where(earlier == slot.astype(F32), named, 0.0)
    sel_out[...] = select.astype(BF16)
    slots = DEPTH * SLOT_ROWS
    picker = select.T[:slots].astype(BF16)
    slot_entry = jnp.sum((select * entry).T[:slots], axis=1, keepdims=True)
    table_at = lax.broadcasted_iota(jnp.int32, (slots, table_ref.shape[1]), 1).astype(F32)
    slot_gate = jnp.sum(jnp.where(table_at == slot_entry, table_ref[...], 0.0), axis=1, keepdims=True)

    loads[0].wait()
    picked_x = jnp.dot(picker, tok[...], preferred_element_type=F32)
    loads[1].wait()
    picked_cot = slot_gate * jnp.dot(picker, cot[...], preferred_element_type=F32)

    def block(k):
        at = slice(k * SLOT_ROWS, (k + 1) * SLOT_ROWS)
        return jnp.concatenate([picked_x[at], picked_cot[at]], axis=0).astype(BF16)

    for k in range(1, DEPTH):
        sbuf[k - 1] = block(k)
    rows[0, 0, 0] = block(0)
    pl.semaphore_wait(barrier, 6)

    def spread(k):
        c_x[k].start()
        c_y[k].start()
        c_p[0][k].start()

    def relay(k):
        c_x[k].wait_recv()
        c_ry[k].start()
        c_p[1][k].start()
        c_y[k].wait_recv()
        c_rx[k].start()
        c_p[2][k].start()

    for k in (3, 1, 2):
        c_z[k].start()
    spread(0)
    for load in loads[2:]:
        load.wait()
    c_z[1].wait_recv()
    spread(1)
    relay(0)
    c_z[2].wait_recv()
    spread(2)
    relay(1)
    c_z[3].wait_recv()
    spread(3)
    relay(2)
    relay(3)

    def piece(q):
        for k in ks_all:
            c_p[q][k].wait_recv()
        pre = lax.dot_general(
            rows[q].reshape(2 * DEPTH * BLOCK, width), w[...],
            (((1,), (1,)), ((), ())), preferred_element_type=F32,
        ).reshape(2 * DEPTH, BLOCK, 3 * units)
        pre_x = pre[:, :SLOT_ROWS].reshape(2 * slots, 3 * units)
        pre_c = pre[:, SLOT_ROWS:].reshape(2 * slots, 3 * units)
        gate, up, hidden_delta = pre_x[:, :units], pre_x[:, units : 2 * units], pre_c[:, 2 * units :]
        sig = jax.nn.sigmoid(gate)
        active = gate * sig
        hidden = active * up
        gate_delta = hidden_delta * up * (sig * (1.0 + gate * (1.0 - sig)))
        up_delta = hidden_delta * active
        both = jnp.concatenate([gate_delta, up_delta], axis=1)
        back = jnp.dot(both.astype(BF16), w[: 2 * units], preferred_element_type=F32)
        pa_s[q] = back[slots:].astype(BF16)
        c_pa[q].start()
        acc[q] = back[:slots]
        none = jnp.zeros((2 * DEPTH, SLOT_ROWS, units), F32)

        def placed(values, first):
            values = values.reshape(2 * DEPTH, SLOT_ROWS, units)
            pair = [values, none] if first else [none, values]
            return jnp.concatenate(pair, axis=1).reshape(2 * DEPTH * BLOCK, units)

        full = jnp.concatenate(
            [placed(gate_delta, True), placed(up_delta, True), placed(hidden, False)], axis=1
        )
        delta[q * 2 * DEPTH * BLOCK : (q + 1) * 2 * DEPTH * BLOCK] = full.astype(BF16)

    piece(0)
    for k in ks_all:
        c_ry[k].wait_recv()
        c_rx[k].wait_recv()
        c_p[3][k].start()
    piece(1)
    piece(2)
    piece(3)

    chunks = wgrad_out.shape[1] // 512
    stores = [
        pltpu.make_async_copy(
            wgrad.at[:, pl.ds(512 * n, 512)], wgrad_out.at[:, pl.ds(512 * n, 512)], out_sem.at[n]
        )
        for n in range(chunks)
    ]

    def weights(n):
        at = slice(512 * n, 512 * (n + 1))
        right = rows[:, :, :, :, at].reshape(PLANE * 2 * DEPTH * BLOCK, 512)
        wgrad[:, at] = lax.dot_general(
            delta[...], right, (((0,), (0,)), ((), ())), preferred_element_type=F32
        ).astype(BF16)
        stores[n].start()

    def merged(q):
        c_pa[q].wait_recv()
        return acc[q] + pa_r[q].astype(F32)

    one = merged(1)
    bx_s[0] = one[:, :half].astype(BF16)
    c_bx[0].start()
    acc[1] = one
    two = merged(2)
    by_s[0] = two[:, half:].astype(BF16)
    c_by[0].start()
    acc[2] = two
    three = merged(3)
    bx_s[1] = three[:, :half].astype(BF16)
    c_bx[1].start()
    by_s[1] = three[:, half:].astype(BF16)
    c_by[1].start()
    acc[0] = merged(0)
    for n in range(0, chunks - 2):
        weights(n)
    c_bx[1].wait_recv()
    cy_s[...] = (acc[2, :, :half] + bx_r[1].astype(F32)).astype(BF16)
    c_cy.start()
    c_by[1].wait_recv()
    cx_s[...] = (acc[1, :, half:] + by_r[1].astype(F32)).astype(BF16)
    c_cx.start()
    weights(chunks - 2)
    c_bx[0].wait_recv()
    c_by[0].wait_recv()
    c_cy.wait_recv()
    c_cx.wait_recv()
    left = acc[0, :, :half] + bx_r[0].astype(F32) + cy_r[...].astype(F32)
    right = acc[0, :, half:] + by_r[0].astype(F32) + cx_r[...].astype(F32)
    for k in (3, 1, 2):
        at = slice(k * SLOT_ROWS, (k + 1) * SLOT_ROWS)
        zs_s[k - 1] = jnp.concatenate([left[at], right[at]], axis=0).astype(BF16)
        c_zs[k].start()
    weights(chunks - 1)
    parts = [jnp.concatenate([left[:SLOT_ROWS], right[:SLOT_ROWS]], axis=1)]
    for k in range(1, DEPTH):
        c_zs[k].wait_recv()
        got = zs_r[k - 1].astype(F32)
        parts.append(jnp.concatenate([got[:SLOT_ROWS], got[SLOT_ROWS:]], axis=1))
    ps_out[...] = jnp.concatenate(parts, axis=0).astype(BF16)

    for copy in c_z[1:] + c_x + c_y + c_rx + c_ry + sum(c_p, []) + c_pa + c_bx + c_by:
        copy.wait_send()
    for copy in [c_cx, c_cy] + c_zs[1:]:
        copy.wait_send()
    for store in stores:
        store.wait()


def per_device_fast(tokens, cotangent, route, gate_index, gate_table, w_gate, w_up, w_down):
    count, width = tokens.shape
    units = w_gate.shape[0]
    half = width // 2
    slots = DEPTH * SLOT_ROWS
    vmem = pl.BlockSpec(memory_space=pltpu.VMEM)
    hbm = pl.BlockSpec(memory_space=pltpu.HBM)
    slot_grads, select, weight_grads = pl.pallas_call(
        kernel,
        out_shape=(
            jax.ShapeDtypeStruct((slots, width), BF16),
            jax.ShapeDtypeStruct((count, 128), BF16),
            jax.ShapeDtypeStruct((3 * units, width), BF16),
        ),
        in_specs=[vmem] * 3 + [hbm] * 5,
        out_specs=(vmem, vmem, pl.BlockSpec(memory_space=pl.ANY)),
        scratch_shapes=[
            pltpu.VMEM((count, width), BF16),
            pltpu.VMEM((count, width), BF16),
            pltpu.VMEM((3 * units, width), BF16),
            pltpu.VMEM((DEPTH - 1, BLOCK, width), BF16),
            pltpu.VMEM((PLANE, 2, DEPTH, BLOCK, width), BF16),
            pltpu.VMEM((PLANE * 2 * DEPTH * BLOCK, 3 * units), BF16),
            pltpu.VMEM((PLANE, slots, width), F32),
            pltpu.VMEM((PLANE, slots, width), BF16),
            pltpu.VMEM((PLANE, slots, width), BF16),
        ]
        + [pltpu.VMEM((2, slots, half), BF16)] * 4
        + [pltpu.VMEM((slots, half), BF16)] * 4
        + [pltpu.VMEM((DEPTH - 1, BLOCK, half), BF16)] * 2
        + [
            pltpu.VMEM((3 * units, width), BF16),
            pltpu.SemaphoreType.DMA((5,)),
            pltpu.SemaphoreType.DMA((width // 512,)),
            pltpu.SemaphoreType.DMA((52,)),
            pltpu.SemaphoreType.DMA((52,)),
        ],
        compiler_params=pltpu.CompilerParams(
            collective_id=0, has_side_effects=True, vmem_limit_bytes=40 * 1024 * 1024
        ),
    )(route, gate_index, gate_table.reshape(1, -1), tokens, cotangent, w_gate, w_up, w_down)
    grad_tokens = jnp.dot(
        select[:, :slots], slot_grads, preferred_element_type=jnp.float32
    ).astype(jnp.bfloat16)
    wide = weight_grads.astype(jnp.float32)
    return (grad_tokens, wide[:units], wide[units : 2 * units], wide[2 * units :])


def solution(mesh):
    one_plane_each = mesh.shape["own"] == DEPTH * PLANE and mesh.shape["rep"] == 2
    body = per_device_fast if one_plane_each else per_device
    return jax.shard_map(
        body,
        mesh=mesh,
        in_specs=(
            P(("own", "rep"), None),
            P(("own", "rep"), None),
            P(("own", "rep"), None),
            P(("own", "rep"), None),
            P(),
            P(("own", "rep"), None),
            P(("own", "rep"), None),
            P(("own", "rep"), None),
        ),
        out_specs=(
            P(("own", "rep"), None),
            P(("own", "rep"), None),
            P(("own", "rep"), None),
            P(("own", "rep"), None),
        ),
        check_vma=False,
    )
```

```python
import jax
import jax.numpy as jnp
from jax import lax
from jax.sharding import PartitionSpec as P

from jax.experimental import pallas as pl
from jax.experimental.pallas import tpu as pltpu

SPLIT = 4
CAP = 6


def silu_parts(pre_gate):
    sigmoid_value = jax.nn.sigmoid(pre_gate)
    return (pre_gate * sigmoid_value, sigmoid_value * (1.0 + pre_gate * (1.0 - sigmoid_value)))


def panel_terms(rows_x, rows_cot, panel_gate, panel_up, panel_down):
    pre_gate = jnp.dot(rows_x, panel_gate.T, preferred_element_type=jnp.float32)
    pre_up = jnp.dot(rows_x, panel_up.T, preferred_element_type=jnp.float32)
    active, slope_value = silu_parts(pre_gate)
    hidden = (active * pre_up).astype(jnp.bfloat16)
    hidden_delta = jnp.dot(rows_cot, panel_down.T, preferred_element_type=jnp.float32)
    gate_delta = (hidden_delta * pre_up * slope_value).astype(jnp.bfloat16)
    up_delta = (hidden_delta * active).astype(jnp.bfloat16)
    grad_rows = jnp.dot(gate_delta, panel_gate, preferred_element_type=jnp.float32) + jnp.dot(
        up_delta, panel_up, preferred_element_type=jnp.float32
    )
    grad_gate = jnp.dot(gate_delta.T, rows_x, preferred_element_type=jnp.float32)
    grad_up = jnp.dot(up_delta.T, rows_x, preferred_element_type=jnp.float32)
    grad_down = jnp.dot(hidden.T, rows_cot, preferred_element_type=jnp.float32)
    return (grad_rows, grad_gate, grad_up, grad_down)


def per_device(tokens, cotangent, route, gate_index, gate_table, w_gate, w_up, w_down):
    owners = lax.axis_size("own")
    experts_here = owners // SPLIT
    tok_count = tokens.shape[0]
    model_width = tokens.shape[1]
    choices_each = route.shape[1]
    table_hits = (
        gate_index[:, :, None] == jnp.arange(gate_table.shape[0], dtype=jnp.int32)[None, None, :]
    ).astype(jnp.float32)
    gate_values = jnp.sum(table_hits * gate_table[None, None, :], axis=2).reshape(-1)
    is_named = (
        route.reshape(-1)[:, None] == jnp.arange(experts_here, dtype=jnp.int32)[None, :]
    ).astype(jnp.int32)
    pair_ids = jnp.arange(is_named.shape[0], dtype=jnp.int32)
    earlier = jnp.dot(
        (pair_ids[:, None] > pair_ids[None, :]).astype(jnp.bfloat16),
        is_named.astype(jnp.bfloat16),
        preferred_element_type=jnp.float32,
    ).astype(jnp.int32)
    slot_hits = (
        is_named[:, :, None]
        * (earlier[:, :, None] == jnp.arange(CAP, dtype=jnp.int32)[None, None, :]).astype(jnp.int32)
    ).astype(jnp.float32)
    slot_hits = slot_hits.reshape(tok_count * choices_each, experts_here * CAP)
    select = slot_hits.reshape(tok_count, choices_each, experts_here * CAP).sum(axis=1)
    slot_gate = jnp.dot(
        gate_values, slot_hits, precision=lax.Precision.HIGHEST, preferred_element_type=jnp.float32
    )
    picker = select.astype(jnp.bfloat16)
    sent_x = jnp.dot(picker.T, tokens, preferred_element_type=jnp.float32).astype(jnp.bfloat16)
    sent_dy = jnp.dot(picker.T, cotangent, preferred_element_type=jnp.float32)
    sent_cot = (slot_gate[:, None] * sent_dy).astype(jnp.bfloat16)

    def fan_out(slot_rows):
        spread = jnp.broadcast_to(
            slot_rows.reshape(experts_here, 1, CAP, model_width),
            (experts_here, SPLIT, CAP, model_width),
        )
        return spread.reshape(owners, CAP, model_width)

    got_x, got_cot = (
        lax.all_to_all(fan_out(sent_x), "own", split_axis=0, concat_axis=0, tiled=True),
        lax.all_to_all(fan_out(sent_cot), "own", split_axis=0, concat_axis=0, tiled=True),
    )
    rows_x = got_x.reshape(owners * CAP, model_width)
    rows_cot = got_cot.reshape(owners * CAP, model_width)
    full_gate, full_up, full_down = (
        lax.all_gather(w_gate, "rep", axis=0, tiled=True),
        lax.all_gather(w_up, "rep", axis=0, tiled=True),
        lax.all_gather(w_down, "rep", axis=0, tiled=True),
    )
    grad_rows, grad_gate, grad_up, grad_down = panel_terms(
        rows_x, rows_cot, full_gate, full_up, full_down
    )
    block_rows = grad_rows.astype(jnp.bfloat16).reshape(owners, CAP, model_width)
    returned = lax.all_to_all(block_rows, "own", split_axis=0, concat_axis=0, tiled=True)
    per_slot = (
        returned.astype(jnp.float32)
        .reshape(experts_here, SPLIT, CAP, model_width)
        .sum(axis=1)
        .reshape(experts_here * CAP, model_width)
    )
    grad_tokens = jnp.dot(
        select, per_slot, precision=lax.Precision.HIGHEST, preferred_element_type=jnp.float32
    ).astype(jnp.bfloat16)
    stacked = jnp.stack([grad_gate, grad_up, grad_down]).astype(jnp.bfloat16).astype(jnp.float32)
    totals_all = lax.psum(stacked.astype(jnp.bfloat16), "rep").astype(jnp.float32)
    rows_each = stacked.shape[1] // lax.axis_size("rep")
    shares = lax.dynamic_slice_in_dim(totals_all, lax.axis_index("rep") * rows_each, rows_each, 1)
    return (grad_tokens, shares[0], shares[1], shares[2])


MESH = pl.DeviceIdType.MESH
F32 = jnp.float32
BF16 = jnp.bfloat16
SLOTS = CAP
SLOT_ROWS = 8
BLOCK = 2 * SLOT_ROWS
PLANE = 4
DEPTH = 4
VMEM_BYTES = 62 * 1024 * 1024


def flip(value, bit):
    return value + bit - 2 * bit * lax.rem(lax.div(value, bit), 2)


def flipped(value, pattern):
    for bit in (1, 2):
        if pattern & bit:
            value = flip(value, bit)
    return value


def kernel(
    route_hbm, gidx_hbm, table_hbm, tok_hbm, cot_hbm, wg_hbm, wu_hbm, wd_hbm,
    tokens_out, wgrad_out,
    route_ref, gidx_ref, table_ref, tok, cot, w, sbuf, rows, tails, delta, acc, pa_s, pa_r, bx_s, bx_r, by_s, by_r,
    cx_s, cx_r, cy_s, cy_r, zs_s, zs_r, wgrad,
    in_sem, out_sem, send_sem, recv_sem,
):
    own = lax.axis_index("own")
    rep = lax.axis_index("rep")
    z = lax.div(own, PLANE)
    s = lax.rem(own, PLANE)
    width = tok.shape[1]
    tail = width // 4
    packed = 3 * tail
    cut = bx_s.shape[2]
    units = wg_hbm.shape[0]

    small = [
        pltpu.make_async_copy(route_hbm, route_ref, in_sem.at[5]),
        pltpu.make_async_copy(gidx_hbm, gidx_ref, in_sem.at[6]),
        pltpu.make_async_copy(table_hbm, table_ref, in_sem.at[7]),
    ]
    loads = [
        pltpu.make_async_copy(tok_hbm, tok, in_sem.at[0]),
        pltpu.make_async_copy(cot_hbm, cot, in_sem.at[1]),
        pltpu.make_async_copy(wg_hbm, w.at[pl.ds(0, units)], in_sem.at[2]),
        pltpu.make_async_copy(wu_hbm, w.at[pl.ds(units, units)], in_sem.at[3]),
        pltpu.make_async_copy(wd_hbm, w.at[pl.ds(2 * units, units)], in_sem.at[4]),
    ]
    for load in small + loads:
        load.start()

    dev_z = [None] + [(flipped(z, k) * PLANE + s, rep) for k in range(1, DEPTH)]
    dev_x = (z * PLANE + flip(s, 1), rep)
    dev_y = (z * PLANE + flip(s, 2), rep)
    dev_p = (own, 1 - rep)
    barrier = pltpu.get_barrier_semaphore()
    for device in dev_z[1:] + [dev_x, dev_y, dev_p]:
        pl.semaphore_signal(barrier, inc=1, device_id=device, device_id_type=MESH)

    number = iter(range(64))

    def remote(src, dst, device):
        i = next(number)
        return pltpu.make_async_remote_copy(
            src_ref=src, dst_ref=dst, send_sem=send_sem.at[i], recv_sem=recv_sem.at[i],
            device_id=device, device_id_type=MESH,
        )

    lo, hi = pl.ds(0, cut), pl.ds(cut, packed - cut)
    ks_all = range(DEPTH)
    c_z = [None] + [remote(sbuf.at[k - 1], rows.at[0, 0, k], dev_z[k]) for k in range(1, DEPTH)]
    c_x = [remote(rows.at[0, 0, k], rows.at[1, 0, k], dev_x) for k in ks_all]
    c_y = [remote(rows.at[0, 0, k], rows.at[2, 0, k], dev_y) for k in ks_all]
    c_rx = [remote(rows.at[2, 0, k, :, hi], rows.at[3, 0, k, :, hi], dev_x) for k in ks_all]
    c_ry = [remote(rows.at[1, 0, k, :, lo], rows.at[3, 0, k, :, lo], dev_y) for k in ks_all]
    c_p = [[remote(rows.at[q, 0, k], rows.at[q, 1, k], dev_p) for k in ks_all] for q in range(PLANE)]
    c_pa = [remote(pa_s.at[q], pa_r.at[q], dev_p) for q in range(PLANE)]
    c_bx = [remote(bx_s.at[q], bx_r.at[q], dev_x) for q in range(2)]
    c_by = [remote(by_s.at[q], by_r.at[q], dev_y) for q in range(2)]
    c_cx = remote(cx_s, cx_r, dev_x)
    c_cy = remote(cy_s, cy_r, dev_y)
    c_zs = [None] + [remote(zs_s.at[k - 1], zs_r.at[k - 1], dev_z[k]) for k in range(1, DEPTH)]

    choices, count = route_ref.shape
    slots = DEPTH * SLOT_ROWS
    line = lax.broadcasted_iota(jnp.int32, (slots, 1), 0)
    which = lax.div(line, SLOT_ROWS)
    slot = lax.rem(line, SLOT_ROWS)
    low, high = lax.rem(which, 2), lax.div(which, 2)
    z_low, z_high = lax.rem(z, 2), lax.div(z, 2)
    expert = (low + z_low - 2 * low * z_low) + 2 * (high + z_high - 2 * high * z_high)
    for load in small:
        load.wait()
    named = jnp.zeros((slots, count), F32)
    entry = jnp.zeros((slots, count), F32)
    for choice in range(choices):
        hit = route_ref[choice : choice + 1, :] == expert
        named = named + jnp.where(hit, 1.0, 0.0)
        entry = entry + jnp.where(hit, gidx_ref[choice : choice + 1, :].astype(F32), 0.0)
    before = (
        lax.broadcasted_iota(jnp.int32, (count, count), 0)
        < lax.broadcasted_iota(jnp.int32, (count, count), 1)
    )
    earlier = jnp.dot(
        named.astype(BF16), jnp.where(before, 1.0, 0.0).astype(BF16), preferred_element_type=F32
    )
    thirds = range(3)
    spare = slot >= SLOTS

    def pick(number, rows_on):
        return jnp.where((earlier == number.astype(F32)) & rows_on, named, 0.0)

    select = pick(slot, slot < SLOTS)
    spill = [pick(3 * (slot - SLOTS) + n, spare) for n in thirds]
    pickers = [jnp.concatenate([select, spill[n]], axis=1).astype(BF16) for n in thirds]
    table_at = lax.broadcasted_iota(jnp.int32, (slots, table_ref.shape[1]), 1).astype(F32)

    def gate_of(n):
        at = jnp.sum((select + spill[n]) * entry, axis=1, keepdims=True)
        return jnp.sum(jnp.where(table_at == at, table_ref[...], 0.0), axis=1, keepdims=True)

    def picked(n, source):
        both = jnp.concatenate([source[:, tail * n : tail * (n + 1)], source[:, packed:]], axis=0)
        return jnp.dot(pickers[n], both, preferred_element_type=F32)

    gates = [gate_of(n) for n in thirds]
    loads[0].wait()
    loads[1].wait()
    for n in thirds:
        cols = slice(tail * n, tail * (n + 1))
        from_x = picked(n, tok)
        from_cot = gates[n] * picked(n, cot)
        for k in ks_all:
            at = slice(k * SLOT_ROWS, (k + 1) * SLOT_ROWS)
            block = jnp.concatenate([from_x[at], from_cot[at]], axis=0).astype(BF16)
            if k == 0:
                rows[0, 0, 0, :, cols] = block
            else:
                sbuf[k - 1, :, cols] = block
    pl.semaphore_wait(barrier, 6)

    def spread(k):
        c_x[k].start()
        c_y[k].start()
        c_p[0][k].start()

    def relay(k):
        c_x[k].wait_recv()
        c_ry[k].start()
        c_p[1][k].start()
        c_y[k].wait_recv()
        c_rx[k].start()
        c_p[2][k].start()

    for k in (1, 3, 2):
        c_z[k].start()
    spread(0)
    c_z[1].wait_recv()
    spread(1)
    relay(0)
    c_z[2].wait_recv()
    spread(2)
    relay(1)
    c_z[3].wait_recv()
    spread(3)
    relay(2)
    relay(3)

    def spill_map(size, transposed):
        to = lax.broadcasted_iota(jnp.int32, (size, size), 1 if transposed else 0)
        at = lax.broadcasted_iota(jnp.int32, (size, size), 0 if transposed else 1)
        same = lax.shift_right_logical(to, 3) == lax.shift_right_logical(at, 3)
        to, at = to & 7, at & 7
        return [
            jnp.where(same & (at >= SLOTS) & (to == 3 * (at - SLOTS) + n), 1.0, 0.0).astype(BF16)
            for n in thirds
        ]

    unspill = spill_map(2 * DEPTH * BLOCK, False)
    respill = spill_map(2 * slots, True)
    held = (lax.broadcasted_iota(jnp.int32, (2 * slots, 1), 0) & 7) < SLOTS
    for load in loads[2:]:
        load.wait()
    across = (((1,), (1,)), ((), ()))

    def piece(q):
        for k in ks_all:
            c_p[q][k].wait_recv()
        size = 2 * DEPTH * BLOCK
        landed = rows[q].reshape(size, packed)
        ends = jnp.zeros((size, tail), F32)
        for n in thirds:
            ends = ends + jnp.dot(
                unspill[n], landed[:, tail * n : tail * (n + 1)], preferred_element_type=F32
            )
        ends = ends.astype(BF16)
        tails[q * size : (q + 1) * size] = ends
        pre = lax.dot_general(landed, w[:, :packed], across, preferred_element_type=F32)
        pre = pre + lax.dot_general(ends, w[:, packed:], across, preferred_element_type=F32)
        pre = pre.reshape(2 * DEPTH, BLOCK, 3 * units)
        pre_x = pre[:, :SLOT_ROWS].reshape(2 * slots, 3 * units)
        pre_c = pre[:, SLOT_ROWS:].reshape(2 * slots, 3 * units)
        gate, up, hidden_delta = pre_x[:, :units], pre_x[:, units : 2 * units], pre_c[:, 2 * units :]
        sig = jax.nn.sigmoid(gate)
        active = gate * sig
        hidden = jnp.where(held, active * up, 0.0)
        gate_delta = hidden_delta * up * (sig * (1.0 + gate * (1.0 - sig)))
        gate_delta = jnp.where(held, gate_delta, 0.0)
        up_delta = jnp.where(held, hidden_delta * active, 0.0)
        both = jnp.concatenate([gate_delta, up_delta], axis=1).astype(BF16)
        for n in thirds:
            cols = slice(tail * n, tail * (n + 1))
            moved = jnp.dot(respill[n], both, preferred_element_type=F32).astype(BF16)
            left = jnp.concatenate([both, moved], axis=1)
            right = jnp.concatenate([w[: 2 * units, cols], w[: 2 * units, packed:]], axis=0)
            back = jnp.dot(left, right, preferred_element_type=F32)
            pa_s[q, :, cols] = back[slots:].astype(BF16)
            acc[q, :, cols] = back[:slots]
        c_pa[q].start()
        none = jnp.zeros((2 * DEPTH, SLOT_ROWS, units), F32)

        def placed(values, first):
            values = values.reshape(2 * DEPTH, SLOT_ROWS, units)
            pair = [values, none] if first else [none, values]
            return jnp.concatenate(pair, axis=1).reshape(2 * DEPTH * BLOCK, units)

        full = jnp.concatenate(
            [placed(gate_delta, True), placed(up_delta, True), placed(hidden, False)], axis=1
        )
        delta[q * 2 * DEPTH * BLOCK : (q + 1) * 2 * DEPTH * BLOCK] = full.astype(BF16)

    piece(0)
    for k in ks_all:
        c_ry[k].wait_recv()
        c_rx[k].wait_recv()
        c_p[3][k].start()
    piece(1)
    piece(2)
    piece(3)

    chunks = 4
    stores = [
        pltpu.make_async_copy(
            wgrad.at[:, pl.ds(tail * n, tail)], wgrad_out.at[:, pl.ds(tail * n, tail)], out_sem.at[n]
        )
        for n in range(chunks)
    ]

    def weights(n):
        at = slice(tail * n, tail * (n + 1))
        right = rows[:, :, :, :, at].reshape(tails.shape) if n < 3 else tails[...]
        wgrad[:, at] = lax.dot_general(
            delta[...], right, (((0,), (0,)), ((), ())), preferred_element_type=F32
        ).astype(BF16)
        stores[n].start()

    def merged(q):
        c_pa[q].wait_recv()
        return acc[q] + pa_r[q].astype(F32)

    one = merged(1)
    bx_s[0] = one[:, :cut].astype(BF16)
    c_bx[0].start()
    acc[1] = one
    two = merged(2)
    by_s[0] = two[:, cut:].astype(BF16)
    c_by[0].start()
    acc[2] = two
    three = merged(3)
    bx_s[1] = three[:, :cut].astype(BF16)
    c_bx[1].start()
    by_s[1] = three[:, cut:].astype(BF16)
    c_by[1].start()
    acc[0] = merged(0)
    for n in range(0, chunks - 2):
        weights(n)
    c_bx[1].wait_recv()
    cy_s[...] = (acc[2, :, :cut] + bx_r[1].astype(F32)).astype(BF16)
    c_cy.start()
    c_by[1].wait_recv()
    cx_s[...] = (acc[1, :, cut:] + by_r[1].astype(F32)).astype(BF16)
    c_cx.start()
    weights(chunks - 2)
    c_bx[0].wait_recv()
    c_by[0].wait_recv()
    c_cy.wait_recv()
    c_cx.wait_recv()
    left = acc[0, :, :cut] + bx_r[0].astype(F32) + cy_r[...].astype(F32)
    right = acc[0, :, cut:] + by_r[0].astype(F32) + cx_r[...].astype(F32)
    filler = jnp.zeros((SLOT_ROWS, 2 * cut - packed), F32)
    for k in (3, 2, 1):
        at = slice(k * SLOT_ROWS, (k + 1) * SLOT_ROWS)
        zs_s[k - 1] = jnp.concatenate([left[at], jnp.concatenate([right[at], filler], axis=1)], axis=0).astype(BF16)
        c_zs[k].start()
    weights(chunks - 1)
    parts = [jnp.concatenate([left[:SLOT_ROWS], right[:SLOT_ROWS]], axis=1)]
    for k in range(1, DEPTH):
        c_zs[k].wait_recv()
        got = zs_r[k - 1].astype(F32)
        parts.append(jnp.concatenate([got[:SLOT_ROWS], got[SLOT_ROWS:, : packed - cut]], axis=1))
    slot_grads = jnp.concatenate(parts, axis=0).astype(BF16)
    down = (((0,), (0,)), ((), ()))
    tokens_out[:, :packed] = lax.dot_general(
        select.astype(BF16), slot_grads, down, preferred_element_type=F32
    ).astype(BF16)
    rest = jnp.zeros((count, tail), F32)
    for n in thirds:
        rest = rest + lax.dot_general(
            spill[n].astype(BF16), slot_grads[:, tail * n : tail * (n + 1)], down,
            preferred_element_type=F32,
        )
    tokens_out[:, packed:] = rest.astype(BF16)

    for copy in c_z[1:] + c_x + c_y + c_rx + c_ry + sum(c_p, []) + c_pa + c_bx + c_by:
        copy.wait_send()
    for copy in [c_cx, c_cy] + c_zs[1:]:
        copy.wait_send()
    for store in stores:
        store.wait()


def per_device_fast(tokens, cotangent, route, gate_index, gate_table, w_gate, w_up, w_down):
    count, width = tokens.shape
    units = w_gate.shape[0]
    packed = width // 4 * 3
    cut = (packed // 128 + 1) // 2 * 128
    slots = DEPTH * SLOT_ROWS
    vmem = pl.BlockSpec(memory_space=pltpu.VMEM)
    hbm = pl.BlockSpec(memory_space=pltpu.HBM)
    grad_tokens, weight_grads = pl.pallas_call(
        kernel,
        out_shape=(
            jax.ShapeDtypeStruct((count, width), BF16),
            jax.ShapeDtypeStruct((3 * units, width), BF16),
        ),
        in_specs=[hbm] * 8,
        out_specs=(vmem, pl.BlockSpec(memory_space=pl.ANY)),
        scratch_shapes=[
            pltpu.VMEM(route.shape[::-1], jnp.int32),
            pltpu.VMEM(route.shape[::-1], jnp.int32),
            pltpu.VMEM((1, gate_table.shape[0]), F32),
            pltpu.VMEM((count, width), BF16),
            pltpu.VMEM((count, width), BF16),
            pltpu.VMEM((3 * units, width), BF16),
            pltpu.VMEM((DEPTH - 1, BLOCK, packed), BF16),
            pltpu.VMEM((PLANE, 2, DEPTH, BLOCK, packed), BF16),
            pltpu.VMEM((PLANE * 2 * DEPTH * BLOCK, width - packed), BF16),
            pltpu.VMEM((PLANE * 2 * DEPTH * BLOCK, 3 * units), BF16),
            pltpu.VMEM((PLANE, slots, packed), F32),
            pltpu.VMEM((PLANE, slots, packed), BF16),
            pltpu.VMEM((PLANE, slots, packed), BF16),
        ]
        + [pltpu.VMEM((2, slots, cut), BF16)] * 2
        + [pltpu.VMEM((2, slots, packed - cut), BF16)] * 2
        + [pltpu.VMEM((slots, packed - cut), BF16)] * 2
        + [pltpu.VMEM((slots, cut), BF16)] * 2
        + [pltpu.VMEM((DEPTH - 1, BLOCK, cut), BF16)] * 2
        + [
            pltpu.VMEM((3 * units, width), BF16),
            pltpu.SemaphoreType.DMA((8,)),
            pltpu.SemaphoreType.DMA((4,)),
            pltpu.SemaphoreType.DMA((52,)),
            pltpu.SemaphoreType.DMA((52,)),
        ],
        compiler_params=pltpu.CompilerParams(
            collective_id=0, has_side_effects=True, vmem_limit_bytes=VMEM_BYTES
        ),
    )(route.T, gate_index.T, gate_table.reshape(1, -1), tokens, cotangent, w_gate, w_up, w_down)
    wide = weight_grads.astype(jnp.float32)
    return (grad_tokens, wide[:units], wide[units : 2 * units], wide[2 * units :])


def solution(mesh):
    one_plane_each = mesh.shape["own"] == DEPTH * PLANE and mesh.shape["rep"] == 2
    body = per_device_fast if one_plane_each else per_device
    return jax.shard_map(
        body,
        mesh=mesh,
        in_specs=(
            P(("own", "rep"), None),
            P(("own", "rep"), None),
            P(("own", "rep"), None),
            P(("own", "rep"), None),
            P(),
            P(("own", "rep"), None),
            P(("own", "rep"), None),
            P(("own", "rep"), None),
        ),
        out_specs=(
            P(("own", "rep"), None),
            P(("own", "rep"), None),
            P(("own", "rep"), None),
            P(("own", "rep"), None),
        ),
        check_vma=False,
    )
```

```python
import jax
import jax.numpy as jnp
from jax import lax
from jax.sharding import PartitionSpec as P

from jax.experimental import pallas as pl
from jax.experimental.pallas import tpu as pltpu

SPLIT = 4
CAP = 6


def silu_parts(pre_gate):
    sigmoid_value = jax.nn.sigmoid(pre_gate)
    return (pre_gate * sigmoid_value, sigmoid_value * (1.0 + pre_gate * (1.0 - sigmoid_value)))


def panel_terms(rows_x, rows_cot, panel_gate, panel_up, panel_down):
    pre_gate = jnp.dot(rows_x, panel_gate.T, preferred_element_type=jnp.float32)
    pre_up = jnp.dot(rows_x, panel_up.T, preferred_element_type=jnp.float32)
    active, slope_value = silu_parts(pre_gate)
    hidden = (active * pre_up).astype(jnp.bfloat16)
    hidden_delta = jnp.dot(rows_cot, panel_down.T, preferred_element_type=jnp.float32)
    gate_delta = (hidden_delta * pre_up * slope_value).astype(jnp.bfloat16)
    up_delta = (hidden_delta * active).astype(jnp.bfloat16)
    grad_rows = jnp.dot(gate_delta, panel_gate, preferred_element_type=jnp.float32) + jnp.dot(
        up_delta, panel_up, preferred_element_type=jnp.float32
    )
    grad_gate = jnp.dot(gate_delta.T, rows_x, preferred_element_type=jnp.float32)
    grad_up = jnp.dot(up_delta.T, rows_x, preferred_element_type=jnp.float32)
    grad_down = jnp.dot(hidden.T, rows_cot, preferred_element_type=jnp.float32)
    return (grad_rows, grad_gate, grad_up, grad_down)


def per_device(tokens, cotangent, route, gate_index, gate_table, w_gate, w_up, w_down):
    owners = lax.axis_size("own")
    experts_here = owners // SPLIT
    tok_count = tokens.shape[0]
    model_width = tokens.shape[1]
    choices_each = route.shape[1]
    table_hits = (
        gate_index[:, :, None] == jnp.arange(gate_table.shape[0], dtype=jnp.int32)[None, None, :]
    ).astype(jnp.float32)
    gate_values = jnp.sum(table_hits * gate_table[None, None, :], axis=2).reshape(-1)
    is_named = (
        route.reshape(-1)[:, None] == jnp.arange(experts_here, dtype=jnp.int32)[None, :]
    ).astype(jnp.int32)
    pair_ids = jnp.arange(is_named.shape[0], dtype=jnp.int32)
    earlier = jnp.dot(
        (pair_ids[:, None] > pair_ids[None, :]).astype(jnp.bfloat16),
        is_named.astype(jnp.bfloat16),
        preferred_element_type=jnp.float32,
    ).astype(jnp.int32)
    slot_hits = (
        is_named[:, :, None]
        * (earlier[:, :, None] == jnp.arange(CAP, dtype=jnp.int32)[None, None, :]).astype(jnp.int32)
    ).astype(jnp.float32)
    slot_hits = slot_hits.reshape(tok_count * choices_each, experts_here * CAP)
    select = slot_hits.reshape(tok_count, choices_each, experts_here * CAP).sum(axis=1)
    slot_gate = jnp.dot(
        gate_values, slot_hits, precision=lax.Precision.HIGHEST, preferred_element_type=jnp.float32
    )
    picker = select.astype(jnp.bfloat16)
    sent_x = jnp.dot(picker.T, tokens, preferred_element_type=jnp.float32).astype(jnp.bfloat16)
    sent_dy = jnp.dot(picker.T, cotangent, preferred_element_type=jnp.float32)
    sent_cot = (slot_gate[:, None] * sent_dy).astype(jnp.bfloat16)

    def fan_out(slot_rows):
        spread = jnp.broadcast_to(
            slot_rows.reshape(experts_here, 1, CAP, model_width),
            (experts_here, SPLIT, CAP, model_width),
        )
        return spread.reshape(owners, CAP, model_width)

    got_x, got_cot = (
        lax.all_to_all(fan_out(sent_x), "own", split_axis=0, concat_axis=0, tiled=True),
        lax.all_to_all(fan_out(sent_cot), "own", split_axis=0, concat_axis=0, tiled=True),
    )
    rows_x = got_x.reshape(owners * CAP, model_width)
    rows_cot = got_cot.reshape(owners * CAP, model_width)
    full_gate, full_up, full_down = (
        lax.all_gather(w_gate, "rep", axis=0, tiled=True),
        lax.all_gather(w_up, "rep", axis=0, tiled=True),
        lax.all_gather(w_down, "rep", axis=0, tiled=True),
    )
    grad_rows, grad_gate, grad_up, grad_down = panel_terms(
        rows_x, rows_cot, full_gate, full_up, full_down
    )
    block_rows = grad_rows.astype(jnp.bfloat16).reshape(owners, CAP, model_width)
    returned = lax.all_to_all(block_rows, "own", split_axis=0, concat_axis=0, tiled=True)
    per_slot = (
        returned.astype(jnp.float32)
        .reshape(experts_here, SPLIT, CAP, model_width)
        .sum(axis=1)
        .reshape(experts_here * CAP, model_width)
    )
    grad_tokens = jnp.dot(
        select, per_slot, precision=lax.Precision.HIGHEST, preferred_element_type=jnp.float32
    ).astype(jnp.bfloat16)
    stacked = jnp.stack([grad_gate, grad_up, grad_down]).astype(jnp.bfloat16).astype(jnp.float32)
    totals_all = lax.psum(stacked.astype(jnp.bfloat16), "rep").astype(jnp.float32)
    rows_each = stacked.shape[1] // lax.axis_size("rep")
    shares = lax.dynamic_slice_in_dim(totals_all, lax.axis_index("rep") * rows_each, rows_each, 1)
    return (grad_tokens, shares[0], shares[1], shares[2])


MESH = pl.DeviceIdType.MESH
F32 = jnp.float32
BF16 = jnp.bfloat16
SLOTS = CAP
SLOT_ROWS = 8
BLOCK = 2 * SLOT_ROWS
PLANE = 4
DEPTH = 4
VMEM_BYTES = 62 * 1024 * 1024


def flip(value, bit):
    return value + bit - 2 * bit * lax.rem(lax.div(value, bit), 2)


def flipped(value, pattern):
    for bit in (1, 2):
        if pattern & bit:
            value = flip(value, bit)
    return value


def kernel(
    route_hbm, gidx_hbm, table_hbm, tok_hbm, cot_hbm, wg_hbm, wu_hbm, wd_hbm,
    tokens_out, wgrad_out,
    route_ref, gidx_ref, table_ref, tok, cot, w, sbuf, rows, tails, delta, acc, pa_s, pa_r, bx_s, bx_r, by_s, by_r,
    cx_s, cx_r, cy_s, cy_r, zs_s, zs_r, wgrad,
    in_sem, out_sem, send_sem, recv_sem,
):
    own = lax.axis_index("own")
    rep = lax.axis_index("rep")
    z = lax.div(own, PLANE)
    s = lax.rem(own, PLANE)
    width = tok.shape[1]
    tail = width // 4
    packed = 3 * tail
    cut = bx_s.shape[2]
    units = wg_hbm.shape[0]

    small = [
        pltpu.make_async_copy(route_hbm, route_ref, in_sem.at[5]),
        pltpu.make_async_copy(gidx_hbm, gidx_ref, in_sem.at[6]),
        pltpu.make_async_copy(table_hbm, table_ref, in_sem.at[7]),
    ]
    loads = [
        pltpu.make_async_copy(tok_hbm, tok, in_sem.at[0]),
        pltpu.make_async_copy(cot_hbm, cot, in_sem.at[1]),
        pltpu.make_async_copy(wg_hbm, w.at[pl.ds(0, units)], in_sem.at[2]),
        pltpu.make_async_copy(wu_hbm, w.at[pl.ds(units, units)], in_sem.at[3]),
        pltpu.make_async_copy(wd_hbm, w.at[pl.ds(2 * units, units)], in_sem.at[4]),
    ]
    for load in small + loads:
        load.start()

    dev_z = [None] + [(flipped(z, k) * PLANE + s, rep) for k in range(1, DEPTH)]
    dev_x = (z * PLANE + flip(s, 1), rep)
    dev_y = (z * PLANE + flip(s, 2), rep)
    dev_p = (own, 1 - rep)
    barrier = pltpu.get_barrier_semaphore()
    for device in dev_z[1:] + [dev_x, dev_y, dev_p]:
        pl.semaphore_signal(barrier, inc=1, device_id=device, device_id_type=MESH)

    number = iter(range(64))

    def remote(src, dst, device):
        i = next(number)
        return pltpu.make_async_remote_copy(
            src_ref=src, dst_ref=dst, send_sem=send_sem.at[i], recv_sem=recv_sem.at[i],
            device_id=device, device_id_type=MESH,
        )

    lo, hi = pl.ds(0, cut), pl.ds(cut, packed - cut)
    ks_all = range(DEPTH)
    c_z = [None] + [remote(sbuf.at[k - 1], rows.at[0, 0, k], dev_z[k]) for k in range(1, DEPTH)]
    c_x = [remote(rows.at[0, 0, k], rows.at[1, 0, k], dev_x) for k in ks_all]
    c_y = [remote(rows.at[0, 0, k], rows.at[2, 0, k], dev_y) for k in ks_all]
    c_rx = [remote(rows.at[2, 0, k, :, hi], rows.at[3, 0, k, :, hi], dev_x) for k in ks_all]
    c_ry = [remote(rows.at[1, 0, k, :, lo], rows.at[3, 0, k, :, lo], dev_y) for k in ks_all]
    c_p = [[remote(rows.at[q, 0, k], rows.at[q, 1, k], dev_p) for k in ks_all] for q in range(PLANE)]
    c_pa = [remote(pa_s.at[q], pa_r.at[q], dev_p) for q in range(PLANE)]
    c_bx = [remote(bx_s.at[q], bx_r.at[q], dev_x) for q in range(2)]
    c_by = [remote(by_s.at[q], by_r.at[q], dev_y) for q in range(2)]
    c_cx = remote(cx_s, cx_r, dev_x)
    c_cy = remote(cy_s, cy_r, dev_y)
    c_zs = [None] + [remote(zs_s.at[k - 1], zs_r.at[k - 1], dev_z[k]) for k in range(1, DEPTH)]

    choices, count = route_ref.shape
    slots = DEPTH * SLOT_ROWS
    line = lax.broadcasted_iota(jnp.int32, (slots, 1), 0)
    which = lax.div(line, SLOT_ROWS)
    slot = lax.rem(line, SLOT_ROWS)
    low, high = lax.rem(which, 2), lax.div(which, 2)
    z_low, z_high = lax.rem(z, 2), lax.div(z, 2)
    expert = (low + z_low - 2 * low * z_low) + 2 * (high + z_high - 2 * high * z_high)
    for load in small:
        load.wait()
    named = jnp.zeros((slots, count), F32)
    entry = jnp.zeros((slots, count), F32)
    for choice in range(choices):
        hit = route_ref[choice : choice + 1, :] == expert
        named = named + jnp.where(hit, 1.0, 0.0)
        entry = entry + jnp.where(hit, gidx_ref[choice : choice + 1, :].astype(F32), 0.0)
    before = (
        lax.broadcasted_iota(jnp.int32, (count, count), 0)
        < lax.broadcasted_iota(jnp.int32, (count, count), 1)
    )
    earlier = jnp.dot(
        named.astype(BF16), jnp.where(before, 1.0, 0.0).astype(BF16), preferred_element_type=F32
    )
    thirds = range(3)
    spare = slot >= SLOTS

    def pick(number, rows_on):
        return jnp.where((earlier == number.astype(F32)) & rows_on, named, 0.0)

    select = pick(slot, slot < SLOTS)
    spill = [pick(3 * (slot - SLOTS) + n, spare) for n in thirds]
    pickers = [jnp.concatenate([select, spill[n]], axis=1).astype(BF16) for n in thirds]
    table_at = lax.broadcasted_iota(jnp.int32, (slots, table_ref.shape[1]), 1).astype(F32)

    def gate_of(n):
        at = jnp.sum((select + spill[n]) * entry, axis=1, keepdims=True)
        return jnp.sum(jnp.where(table_at == at, table_ref[...], 0.0), axis=1, keepdims=True)

    def picked(n, source):
        both = jnp.concatenate([source[:, tail * n : tail * (n + 1)], source[:, packed:]], axis=0)
        return jnp.dot(pickers[n], both, preferred_element_type=F32)

    gates = [gate_of(n) for n in thirds]
    loads[0].wait()
    loads[1].wait()
    for n in thirds:
        cols = slice(tail * n, tail * (n + 1))
        from_x = picked(n, tok)
        from_cot = gates[n] * picked(n, cot)
        for k in ks_all:
            at = slice(k * SLOT_ROWS, (k + 1) * SLOT_ROWS)
            block = jnp.concatenate([from_x[at], from_cot[at]], axis=0).astype(BF16)
            if k == 0:
                rows[0, 0, 0, :, cols] = block
            else:
                sbuf[k - 1, :, cols] = block
    pl.semaphore_wait(barrier, 6)

    def spread(k):
        c_x[k].start()
        c_y[k].start()
        c_p[0][k].start()

    def relay(k):
        c_x[k].wait_recv()
        c_ry[k].start()
        c_p[1][k].start()
        c_y[k].wait_recv()
        c_rx[k].start()
        c_p[2][k].start()

    for k in (1, 3, 2):
        c_z[k].start()
    spread(0)
    c_z[1].wait_recv()
    spread(1)
    relay(0)
    c_z[2].wait_recv()
    spread(2)
    relay(1)
    c_z[3].wait_recv()
    spread(3)
    relay(2)
    relay(3)

    def spill_map(size, transposed):
        to = lax.broadcasted_iota(jnp.int32, (size, size), 1 if transposed else 0)
        at = lax.broadcasted_iota(jnp.int32, (size, size), 0 if transposed else 1)
        same = lax.shift_right_logical(to, 3) == lax.shift_right_logical(at, 3)
        to, at = to & 7, at & 7
        return [
            jnp.where(same & (at >= SLOTS) & (to == 3 * (at - SLOTS) + n), 1.0, 0.0).astype(BF16)
            for n in thirds
        ]

    unspill = spill_map(2 * DEPTH * BLOCK, False)
    respill = spill_map(2 * slots, True)
    held = (lax.broadcasted_iota(jnp.int32, (2 * slots, 1), 0) & 7) < SLOTS
    for load in loads[2:]:
        load.wait()
    across = (((1,), (1,)), ((), ()))

    def piece(q):
        for k in ks_all:
            c_p[q][k].wait_recv()
        size = 2 * DEPTH * BLOCK
        landed = rows[q].reshape(size, packed)
        ends = jnp.zeros((size, tail), F32)
        for n in thirds:
            ends = ends + jnp.dot(
                unspill[n], landed[:, tail * n : tail * (n + 1)], preferred_element_type=F32
            )
        ends = ends.astype(BF16)
        tails[q * size : (q + 1) * size] = ends
        pre = lax.dot_general(landed, w[:, :packed], across, preferred_element_type=F32)
        pre = pre + lax.dot_general(ends, w[:, packed:], across, preferred_element_type=F32)
        pre = pre.reshape(2 * DEPTH, BLOCK, 3 * units)
        pre_x = pre[:, :SLOT_ROWS].reshape(2 * slots, 3 * units)
        pre_c = pre[:, SLOT_ROWS:].reshape(2 * slots, 3 * units)
        gate, up, hidden_delta = pre_x[:, :units], pre_x[:, units : 2 * units], pre_c[:, 2 * units :]
        sig = jax.nn.sigmoid(gate)
        active = gate * sig
        hidden = jnp.where(held, active * up, 0.0)
        gate_delta = hidden_delta * up * (sig * (1.0 + gate * (1.0 - sig)))
        gate_delta = jnp.where(held, gate_delta, 0.0)
        up_delta = jnp.where(held, hidden_delta * active, 0.0)
        both = jnp.concatenate([gate_delta, up_delta], axis=1).astype(BF16)
        for n in thirds:
            cols = slice(tail * n, tail * (n + 1))
            moved = jnp.dot(respill[n], both, preferred_element_type=F32).astype(BF16)
            left = jnp.concatenate([both, moved], axis=1)
            right = jnp.concatenate([w[: 2 * units, cols], w[: 2 * units, packed:]], axis=0)
            back = jnp.dot(left, right, preferred_element_type=F32)
            pa_s[q, :, cols] = back[slots:].astype(BF16)
            acc[q, :, cols] = back[:slots]
        c_pa[q].start()
        none = jnp.zeros((2 * DEPTH, SLOT_ROWS, units), F32)

        def placed(values, first):
            values = values.reshape(2 * DEPTH, SLOT_ROWS, units)
            pair = [values, none] if first else [none, values]
            return jnp.concatenate(pair, axis=1).reshape(2 * DEPTH * BLOCK, units)

        full = jnp.concatenate(
            [placed(gate_delta, True), placed(up_delta, True), placed(hidden, False)], axis=1
        )
        delta[q * 2 * DEPTH * BLOCK : (q + 1) * 2 * DEPTH * BLOCK] = full.astype(BF16)

    piece(0)
    for k in ks_all:
        c_ry[k].wait_recv()
        c_rx[k].wait_recv()
        c_p[3][k].start()
    piece(1)
    piece(2)

    def merged(q):
        c_pa[q].wait_recv()
        return acc[q] + pa_r[q].astype(F32)

    one = merged(1)
    bx_s[0] = one[:, :cut].astype(BF16)
    c_bx[0].start()
    acc[1] = one
    two = merged(2)
    by_s[0] = two[:, cut:].astype(BF16)
    c_by[0].start()
    acc[2] = two
    piece(3)

    chunks = 4
    stores = [
        pltpu.make_async_copy(
            wgrad.at[:, pl.ds(tail * n, tail)], wgrad_out.at[:, pl.ds(tail * n, tail)], out_sem.at[n]
        )
        for n in range(chunks)
    ]

    def weights(n):
        at = slice(tail * n, tail * (n + 1))
        right = rows[:, :, :, :, at].reshape(tails.shape) if n < 3 else tails[...]
        wgrad[:, at] = lax.dot_general(
            delta[...], right, (((0,), (0,)), ((), ())), preferred_element_type=F32
        ).astype(BF16)
        stores[n].start()

    three = merged(3)
    bx_s[1] = three[:, :cut].astype(BF16)
    c_bx[1].start()
    by_s[1] = three[:, cut:].astype(BF16)
    c_by[1].start()
    acc[0] = merged(0)
    for n in range(0, chunks - 2):
        weights(n)
    c_bx[1].wait_recv()
    cy_s[...] = (acc[2, :, :cut] + bx_r[1].astype(F32)).astype(BF16)
    c_cy.start()
    c_by[1].wait_recv()
    cx_s[...] = (acc[1, :, cut:] + by_r[1].astype(F32)).astype(BF16)
    c_cx.start()
    weights(chunks - 2)
    c_bx[0].wait_recv()
    c_by[0].wait_recv()
    c_cy.wait_recv()
    c_cx.wait_recv()
    left = acc[0, :, :cut] + bx_r[0].astype(F32) + cy_r[...].astype(F32)
    right = acc[0, :, cut:] + by_r[0].astype(F32) + cx_r[...].astype(F32)
    filler = jnp.zeros((SLOT_ROWS, 2 * cut - packed), F32)
    for k in (3, 2, 1):
        at = slice(k * SLOT_ROWS, (k + 1) * SLOT_ROWS)
        zs_s[k - 1] = jnp.concatenate([left[at], jnp.concatenate([right[at], filler], axis=1)], axis=0).astype(BF16)
        c_zs[k].start()
    weights(chunks - 1)
    parts = [jnp.concatenate([left[:SLOT_ROWS], right[:SLOT_ROWS]], axis=1)]
    for k in range(1, DEPTH):
        c_zs[k].wait_recv()
        got = zs_r[k - 1].astype(F32)
        parts.append(jnp.concatenate([got[:SLOT_ROWS], got[SLOT_ROWS:, : packed - cut]], axis=1))
    slot_grads = jnp.concatenate(parts, axis=0).astype(BF16)
    down = (((0,), (0,)), ((), ()))
    tokens_out[:, :packed] = lax.dot_general(
        select.astype(BF16), slot_grads, down, preferred_element_type=F32
    ).astype(BF16)
    rest = jnp.zeros((count, tail), F32)
    for n in thirds:
        rest = rest + lax.dot_general(
            spill[n].astype(BF16), slot_grads[:, tail * n : tail * (n + 1)], down,
            preferred_element_type=F32,
        )
    tokens_out[:, packed:] = rest.astype(BF16)

    for copy in c_z[1:] + c_x + c_y + c_rx + c_ry + sum(c_p, []) + c_pa + c_bx + c_by:
        copy.wait_send()
    for copy in [c_cx, c_cy] + c_zs[1:]:
        copy.wait_send()
    for store in stores:
        store.wait()


def per_device_fast(tokens, cotangent, route, gate_index, gate_table, w_gate, w_up, w_down):
    count, width = tokens.shape
    units = w_gate.shape[0]
    packed = width // 4 * 3
    cut = (packed // 128 + 1) // 2 * 128
    slots = DEPTH * SLOT_ROWS
    vmem = pl.BlockSpec(memory_space=pltpu.VMEM)
    hbm = pl.BlockSpec(memory_space=pltpu.HBM)
    grad_tokens, weight_grads = pl.pallas_call(
        kernel,
        out_shape=(
            jax.ShapeDtypeStruct((count, width), BF16),
            jax.ShapeDtypeStruct((3 * units, width), BF16),
        ),
        in_specs=[hbm] * 8,
        out_specs=(vmem, pl.BlockSpec(memory_space=pl.ANY)),
        scratch_shapes=[
            pltpu.VMEM(route.shape[::-1], jnp.int32),
            pltpu.VMEM(route.shape[::-1], jnp.int32),
            pltpu.VMEM((1, gate_table.shape[0]), F32),
            pltpu.VMEM((count, width), BF16),
            pltpu.VMEM((count, width), BF16),
            pltpu.VMEM((3 * units, width), BF16),
            pltpu.VMEM((DEPTH - 1, BLOCK, packed), BF16),
            pltpu.VMEM((PLANE, 2, DEPTH, BLOCK, packed), BF16),
            pltpu.VMEM((PLANE * 2 * DEPTH * BLOCK, width - packed), BF16),
            pltpu.VMEM((PLANE * 2 * DEPTH * BLOCK, 3 * units), BF16),
            pltpu.VMEM((PLANE, slots, packed), F32),
            pltpu.VMEM((PLANE, slots, packed), BF16),
            pltpu.VMEM((PLANE, slots, packed), BF16),
        ]
        + [pltpu.VMEM((2, slots, cut), BF16)] * 2
        + [pltpu.VMEM((2, slots, packed - cut), BF16)] * 2
        + [pltpu.VMEM((slots, packed - cut), BF16)] * 2
        + [pltpu.VMEM((slots, cut), BF16)] * 2
        + [pltpu.VMEM((DEPTH - 1, BLOCK, cut), BF16)] * 2
        + [
            pltpu.VMEM((3 * units, width), BF16),
            pltpu.SemaphoreType.DMA((8,)),
            pltpu.SemaphoreType.DMA((4,)),
            pltpu.SemaphoreType.DMA((52,)),
            pltpu.SemaphoreType.DMA((52,)),
        ],
        compiler_params=pltpu.CompilerParams(
            collective_id=0, has_side_effects=True, vmem_limit_bytes=VMEM_BYTES
        ),
    )(route.T, gate_index.T, gate_table.reshape(1, -1), tokens, cotangent, w_gate, w_up, w_down)
    wide = weight_grads.astype(jnp.float32)
    return (grad_tokens, wide[:units], wide[units : 2 * units], wide[2 * units :])


def solution(mesh):
    one_plane_each = mesh.shape["own"] == DEPTH * PLANE and mesh.shape["rep"] == 2
    body = per_device_fast if one_plane_each else per_device
    return jax.shard_map(
        body,
        mesh=mesh,
        in_specs=(
            P(("own", "rep"), None),
            P(("own", "rep"), None),
            P(("own", "rep"), None),
            P(("own", "rep"), None),
            P(),
            P(("own", "rep"), None),
            P(("own", "rep"), None),
            P(("own", "rep"), None),
        ),
        out_specs=(
            P(("own", "rep"), None),
            P(("own", "rep"), None),
            P(("own", "rep"), None),
            P(("own", "rep"), None),
        ),
        check_vma=False,
    )
```
